32 devices in a mesh: frag: 2 (over x), col: 16 (over z, y, core).
Axes of the slice: x: 2, y: 2, z: 4, core: 2. Of those that a mesh axis runs over, the one named last changes fastest.
Arguments:
- amplitudes: bfloat16 [64, 256, 256], P(('frag', 'col')), parts along dimension 0, may hold values from -6 to 6
- integrals: bfloat16 [64, 256, 256], P(('frag', 'col')), parts along dimension 0, may hold values from -6 to 6
- energies: float32 [64, 256], P(('frag', 'col')), parts along dimension 0, may hold values from 0.5 to 4
- pno_size: int32 [64], P(('frag', 'col')), parts along dimension 0, may hold values from 128 to 256, as said below
- subspace_transfers: bfloat16 [2048, 256, 256], P(('frag', 'col')), parts along dimension 0, may hold values from -0.375 to 0.375
- tile_source: int32 [2048], P(('frag', 'col')), parts along dimension 0, may hold values from 0 to 15
- tile_owner: int32 [2048], P(('frag', 'col')), parts along dimension 0, may hold values from 0 to 15, as said below
- dispatch_table: int32 [32, 16], P('frag'), parts along dimension 0, may hold values from -1 to 1, as said below
- result_list: int32 [32, 16], P('frag'), parts along dimension 0, may hold values from -1 to 1, as said below
Outputs:
- residual: float32 [64, 256, 256], P(('frag', 'col')), parts along dimension 0
The draws below stay inside these ranges and needn't reach their ends.
There are 2 independent parts, one for each index of `frag`. The reference program is written for one: setup_inputs(seed, part) draws one part's arguments, and reference() takes and returns one part's arrays. A program takes and returns all parts, laid end to end along the dimension named above; each array names one. Nothing has to cross between parts.
Inputs may be any that keep to these rules, and one draw needn't show every extreme that they name: `pno_size`: each pair keeps either 256/2 or 256 PNOs. `dispatch_table`: -1 marks a device that couples to no pair of that source device. `result_list`: -1 marks no target pair; entry [d, o] is -1 unless (o - d) mod 16 lies in 1 to 8. `tile_owner`: A tile of device d has an owner o with (o - d) mod 16 in 1 to 8; the first tile of each device has the owner 16/2 away.
All inputs are finite; a program needn't handle non-finite values.
Results may differ from the reference program's by a relative error of at most 0.0075.
Values may be sent and summed in bfloat16 or wider, within the bound.
No kernel may reach another device: no remote copies, remote signals or barrier semaphores. Data moves between devices by JAX's collectives and lax.ppermute only.
A program may use at most 128 MiB of HBM per device.

```python
import math
import jax
import jax.numpy as jnp
from jax import lax

V = 256
PAIR_DEV = 2
TILE_DEV = 64
PAIRS = 32
TILES = 1024
N_COL = 16


def draw_pno_size(key, part):
    key = jax.random.fold_in(key, 11)
    return V // 2 * (1 + jax.random.randint(key, (PAIRS,), 0, 2, dtype=jnp.int32))


def draw_tile_owner(key, part):
    key = jax.random.fold_in(key, 14)
    steps_ahead = jax.random.randint(key, (TILES,), 1, N_COL // 2 + 1, dtype=jnp.int32)
    tile_ids = jnp.arange(TILES, dtype=jnp.int32)
    holders = tile_ids // TILE_DEV
    firsts = tile_ids % TILE_DEV == 0
    steps_ahead = jnp.where(firsts, N_COL // 2, steps_ahead)
    return jnp.mod(holders + steps_ahead, N_COL).astype(jnp.int32)


def draw_dispatch_table(key, part):
    key = jax.random.fold_in(key, 12)
    level_key, live_key, value_key = jax.random.split(key, 3)
    levels = jax.random.randint(level_key, (1, N_COL), 1, 5, dtype=jnp.int32)
    rolls = jax.random.randint(live_key, (N_COL, N_COL), 0, 4, dtype=jnp.int32)
    values = jax.random.randint(value_key, (N_COL, N_COL), 0, PAIR_DEV, dtype=jnp.int32)
    return jnp.where(rolls < levels, values, -1).astype(jnp.int32)


def draw_result_list(key, part):
    key = jax.random.fold_in(key, 13)
    level_key, live_key, value_key = jax.random.split(key, 3)
    levels = jax.random.randint(level_key, (N_COL, 1), 3, 5, dtype=jnp.int32)
    rolls = jax.random.randint(live_key, (N_COL, N_COL), 0, 4, dtype=jnp.int32)
    values = jax.random.randint(value_key, (N_COL, N_COL), 0, PAIR_DEV, dtype=jnp.int32)
    senders = jnp.arange(N_COL, dtype=jnp.int32)[:, None]
    owners = jnp.arange(N_COL, dtype=jnp.int32)[None, :]
    offsets = jnp.mod(owners - senders, N_COL)
    within = (offsets >= 1) & (offsets <= N_COL // 2)
    return jnp.where(within & (rolls < levels), values, -1).astype(jnp.int32)


def place_ends(values, stream_key, smallest, largest):
    place = [jax.random.randint(jax.random.fold_in(stream_key, axis), (), 0, length) for axis, length in enumerate(values.shape)]
    main_axis = values.shape.index(max(values.shape))
    next_to = place[:main_axis] + [(place[main_axis] + 1) % values.shape[main_axis]] + place[main_axis + 1:]
    return values.at[tuple(place)].set(smallest).at[tuple(next_to)].set(largest)


def shard_levels(own_key, shape, shards, low, high):
    def one(position, shards_of):
        heights = jax.random.uniform(jax.random.fold_in(jax.random.fold_in(own_key, 6), position), (shards_of,), jnp.float32, low / len(shards), high / len(shards))
        return jnp.repeat(jnp.exp(heights), shape[position] // shards_of).reshape((-1,) + (1,) * (len(shape) - position - 1))

    factor_of = one(*shards[0])
    for cut in shards[1:]:
        factor_of = factor_of * one(*cut)
    return factor_of


def normal_values(stream_key, extent, spread, bound, pieces=(), kind=jnp.bfloat16):
    entries = jax.random.normal(stream_key, extent, jnp.float32) * spread
    if len(pieces) > 0:
        entries = shard_levels(stream_key, extent, pieces, -0.22, 0.18) * entries
    return jnp.clip(entries, min=-bound, max=bound).astype(kind)


def setup_inputs(seed: int = 0, part: int = 0) -> dict:
    key_list = jax.random.split(jax.random.key(seed), 10)
    own_keys = jax.random.split(jax.random.fold_in(key_list[9], part), 10)
    return {
        "amplitudes": normal_values(own_keys[0], (PAIRS, V, V), 1.0, 6.0, ((0, 16),)),
        "integrals": normal_values(own_keys[1], (PAIRS, V, V), 1.0, 6.0, ((0, 16),)),
        "energies": jnp.clip(jnp.exp(math.log(4.0) - 2.0794415 * jax.random.uniform(own_keys[2], (PAIRS, V), jnp.float32) ** shard_levels(own_keys[2], (PAIRS, V), ((0, 16),), -0.2, 0.2)), 0.5, 4.0),
        "pno_size": draw_pno_size(jax.random.fold_in(jax.random.fold_in(key_list[9], part), 71), part),
        "subspace_transfers": normal_values(own_keys[4], (TILES, V, V), V ** -0.5, 0.375, ((0, 16),)),
        "tile_source": place_ends(jax.random.randint(own_keys[5], (TILES,), 0, N_COL), jax.random.fold_in(own_keys[5], 1), 0, N_COL - 1).astype(jnp.int32),
        "tile_owner": draw_tile_owner(jax.random.fold_in(jax.random.fold_in(key_list[9], part), 71), part),
        "dispatch_table": draw_dispatch_table(jax.random.fold_in(jax.random.fold_in(key_list[9], part), 71), part),
        "result_list": draw_result_list(jax.random.fold_in(jax.random.fold_in(key_list[9], part), 71), part),
    }


def reference(amplitudes, integrals, energies, pno_size, subspace_transfers, tile_source, tile_owner, dispatch_table, result_list):
    lanes = jnp.arange(V, dtype=jnp.int32)
    inside_pno = lanes[None, :] < pno_size[:, None]
    pno_mask = inside_pno[:, :, None] & inside_pno[:, None, :]
    masked = jnp.where(pno_mask, amplitudes, jnp.zeros((), jnp.bfloat16))
    column_ids = jnp.arange(N_COL, dtype=jnp.int32)
    topmost_bound = lax.Precision.HIGHEST

    def visit(running, processor_rank):
        start = (processor_rank * TILE_DEV).astype(jnp.int32)
        patch_subspace_transfers = lax.dynamic_slice_in_dim(subspace_transfers, start, TILE_DEV, 0).astype(jnp.float32)
        sources = lax.dynamic_slice_in_dim(tile_source, start, TILE_DEV, 0)
        owners = lax.dynamic_slice_in_dim(tile_owner, start, TILE_DEV, 0)
        needed = dispatch_table[:, processor_rank]
        given = result_list[processor_rank]
        source_local = needed[sources]
        target_local = given[owners]
        is_live = (source_local >= 0) & (target_local >= 0)
        wanted = (sources * PAIR_DEV + jnp.maximum(source_local, 0)).astype(jnp.int32)
        picked_option = masked[wanted].astype(jnp.float32)
        interim_matrix_result = jnp.einsum("jxq,jqp->jxp", patch_subspace_transfers, picked_option, precision=topmost_bound).astype(jnp.bfloat16)
        interim_matrix_result = lax.optimization_barrier(interim_matrix_result).astype(jnp.float32)
        patch_residual_pieces = jnp.einsum("yzx,ylx->yzl", interim_matrix_result, patch_subspace_transfers, precision=topmost_bound)
        patch_residual_pieces = jnp.where(is_live[:, None, None], patch_residual_pieces, jnp.float32(0.0))
        owner_hot = ((owners[None, :] == column_ids[:, None]) & is_live[None, :]).astype(jnp.float32)
        blocks = jnp.einsum("ot,tab->oab", owner_hot, patch_residual_pieces, precision=topmost_bound).astype(jnp.bfloat16)
        blocks = lax.optimization_barrier(blocks).astype(jnp.float32)
        blocks = jnp.where((given >= 0)[:, None, None], blocks, jnp.float32(0.0))
        target = (column_ids * PAIR_DEV + jnp.maximum(given, 0)).astype(jnp.int32)
        return running.at[target].add(blocks), None

    coupled, _ = lax.scan(visit, jnp.zeros((PAIRS, V, V), jnp.float32), column_ids)
    denominator = energies[:, :, None] + energies[:, None, :]
    result = integrals.astype(jnp.float32) + denominator * masked.astype(jnp.float32) + coupled
    return jnp.where(pno_mask, result, jnp.float32(0.0))
```

```python
import functools

import jax
import jax.numpy as jnp
from jax import lax
from jax.experimental import pallas as pl
from jax.experimental.pallas import tpu as pltpu
from jax.sharding import PartitionSpec as P

GROUP = 4
UNROLL = 4

VMEM = functools.partial(pl.BlockSpec, memory_space=pltpu.VMEM)
SMEM = functools.partial(pl.BlockSpec, memory_space=pltpu.SMEM)
HBM = functools.partial(pl.BlockSpec, memory_space=pl.ANY)


def inside(size, shape):
    rows = lax.broadcasted_iota(jnp.int32, shape, 0)
    lanes = lax.broadcasted_iota(jnp.int32, shape, 1)
    return (rows < size) & (lanes < size)


def mask_kernel(size_ref, amplitude_ref, masked_ref):
    for p in range(masked_ref.shape[0]):
        held = inside(size_ref[p], masked_ref.shape[1:])
        value = jnp.where(held, amplitude_ref[p].astype(jnp.float32), 0.0)
        masked_ref[p] = value.astype(masked_ref.dtype)


def base_kernel(size_ref, energy_ref, integral_ref, masked_ref, base_ref):
    shape = base_ref.shape[1:]
    for p in range(base_ref.shape[0]):
        across = jnp.broadcast_to(energy_ref[p : p + 1, :], shape)
        denominator = across.T + across
        value = integral_ref[p].astype(jnp.float32) + denominator * masked_ref[p].astype(jnp.float32)
        base_ref[p] = jnp.where(inside(size_ref[p], shape), value, 0.0)


def list_kernel(columns, pairs, me_ref, source_ref, owner_ref, dispatch_ref, result_ref, list_ref):
    tiles = source_ref.shape[0]
    depth = columns // GROUP
    half = depth // 2
    me = me_ref[0]
    z, g = me // GROUP, me % GROUP

    def fill(i, _):
        list_ref[0, i] = 0
        list_ref[1, i] = 0
        list_ref[2, i] = columns // 2
        return 0

    lax.fori_loop(0, tiles, fill, 0)

    def visit(t, count):
        s, o = source_ref[t], owner_ref[t]
        pair = dispatch_ref[s, me]
        live = (pair >= 0) & (result_ref[me, o] >= 0)

        @pl.when(live)
        def _():
            far = (s // GROUP - z + depth) % depth
            ahead = (o // GROUP - z + depth) % half
            list_ref[0, count] = t
            list_ref[1, count] = (far * GROUP + (g ^ (s % GROUP))) * pairs + jnp.maximum(pair, 0)
            list_ref[2, count] = ahead * GROUP + (g ^ (o % GROUP))

        return count + live.astype(jnp.int32)

    count = lax.fori_loop(0, tiles, visit, jnp.int32(0))
    list_ref[3, 0] = count


def tiles_kernel(list_ref, masked_ref, transfer_ref, block_ref, held, total, arrived):
    count = list_ref[3, 0]
    steps = (count + UNROLL - 1) // UNROLL

    def copy(i):
        return pltpu.make_async_copy(transfer_ref.at[list_ref[0, i]], held.at[i], arrived.at[i])

    def fetch(i, _):
        copy(i).start()
        return 0

    lax.fori_loop(0, steps * UNROLL, fetch, 0)
    total[...] = jnp.zeros_like(total)

    def step(n, _):
        for u in range(UNROLL):
            i = n * UNROLL + u
            copy(i).wait()
            transfer = held[i]
            half = jnp.dot(transfer, masked_ref[list_ref[1, i]], preferred_element_type=jnp.float32)
            total[list_ref[2, i]] += lax.dot_general(
                half.astype(jnp.bfloat16),
                transfer,
                (((1,), (1,)), ((), ())),
                preferred_element_type=jnp.float32,
            )
        return 0

    lax.fori_loop(0, steps, step, 0)
    for b in range(block_ref.shape[0]):
        block_ref[b] = total[b].astype(block_ref.dtype)


def shards(
    amplitudes,
    integrals,
    energies,
    pno_size,
    subspace_transfers,
    tile_source,
    tile_owner,
    dispatch_table,
    result_list,
):
    pairs, width = amplitudes.shape[:2]
    tiles = subspace_transfers.shape[0]
    columns = lax.axis_size("col")
    depth = columns // GROUP
    half = depth // 2
    me = lax.axis_index("col").astype(jnp.int32)
    z, g = me // GROUP, me % GROUP

    def swap(value, m):
        return lax.ppermute(value, "col", [(i, i ^ m) for i in range(columns)])

    def ahead(value, steps):
        return lax.ppermute(
            value, "col", [(i, (i + steps * GROUP) % columns) for i in range(columns)]
        )

    masked = pl.pallas_call(
        mask_kernel,
        out_shape=jax.ShapeDtypeStruct(amplitudes.shape, jnp.bfloat16),
        in_specs=[SMEM(), VMEM()],
        out_specs=VMEM(),
        name="mask",
    )(pno_size, amplitudes)

    lane = [masked] + [ahead(masked, -far) for far in range(1, depth)]
    across = [swap(part, 2) for part in lane]
    both = [jnp.stack([a, b]) for a, b in zip(lane, across)]
    other = [swap(part, 1) for part in both]
    everyone = jnp.stack(
        [jnp.stack([a[0], b[0], a[1], b[1]]) for a, b in zip(both, other)]
    ).reshape(columns * pairs, width, width)

    tile_list = pl.pallas_call(
        functools.partial(list_kernel, columns, pairs),
        out_shape=jax.ShapeDtypeStruct((4, tiles), jnp.int32),
        in_specs=[SMEM()] * 5,
        out_specs=SMEM(),
        name="tile_list",
    )(me[None], tile_source, tile_owner, dispatch_table, result_list)

    blocks = pl.pallas_call(
        tiles_kernel,
        out_shape=jax.ShapeDtypeStruct((columns // 2, width, width), jnp.bfloat16),
        in_specs=[SMEM(), VMEM(), HBM()],
        out_specs=VMEM(),
        scratch_shapes=[
            pltpu.VMEM((tiles, width, width), jnp.bfloat16),
            pltpu.VMEM((columns // 2 + 1, width, width), jnp.float32),
            pltpu.SemaphoreType.DMA((tiles,)),
        ],
        compiler_params=pltpu.CompilerParams(vmem_limit_bytes=48 * 2**20),
        cost_estimate=pl.CostEstimate(
            flops=4 * tiles * width**3, bytes_accessed=2 * tiles * width**2, transcendentals=0
        ),
        name="tiles",
    )(tile_list, everyone, subspace_transfers)

    def given(steps, m):
        return result_list[z * GROUP + (g ^ m), (z + steps) % depth * GROUP + g]

    def of_pair(parts, p):
        terms = [jnp.where(pair == p, part.astype(jnp.float32), 0.0) for pair, part in parts]
        return functools.reduce(jnp.add, terms)

    coupled = []
    for row in range(half):
        block = [blocks[row * GROUP + m] for m in range(GROUP)]
        block = [block[0]] + [swap(block[m], m) for m in range(1, GROUP)]
        onward = []
        for m in range(GROUP):
            pair = given(row, m)
            if row == 0:
                near = (g ^ m) < g
                stays = jnp.where(near, pair, -1)
                pair = jnp.where(near, -1, given(half, m))
                coupled.append((stays, block[m]))
            onward.append((pair, block[m]))
        sums = jnp.stack([of_pair(onward, p) for p in range(pairs)]).astype(jnp.bfloat16)
        coupled.append((None, ahead(sums, row if row else half)))

    base = pl.pallas_call(
        base_kernel,
        out_shape=jax.ShapeDtypeStruct(amplitudes.shape, jnp.float32),
        in_specs=[SMEM(), VMEM(), VMEM(), VMEM()],
        out_specs=VMEM(),
        name="base",
    )(pno_size, energies, integrals, masked)

    near = [part for part in coupled if part[0] is not None]
    far = [part.astype(jnp.float32) for pair, part in coupled if pair is None]
    total = base + jnp.stack([of_pair(near, p) for p in range(pairs)])
    total = functools.reduce(jnp.add, far, total)
    lanes = jnp.arange(width, dtype=jnp.int32)
    held = lanes[None, :] < pno_size[:, None]
    return jnp.where(held[:, :, None] & held[:, None, :], total, 0.0)


def solution(mesh):
    placed = (
        P(("frag", "col"), None, None),
        P(("frag", "col"), None, None),
        P(("frag", "col"), None),
        P(("frag", "col")),
        P(("frag", "col"), None, None),
        P(("frag", "col")),
        P(("frag", "col")),
        P("frag", None),
        P("frag", None),
    )
    return jax.shard_map(
        shards,
        mesh=mesh,
        in_specs=placed,
        out_specs=P(("frag", "col"), None, None),
        check_vma=False,
    )
```

```python
import functools

import jax
import jax.numpy as jnp
from jax import lax
from jax.experimental import pallas as pl
from jax.experimental.pallas import tpu as pltpu
from jax.sharding import PartitionSpec as P

GROUP = 4
UNROLL = 8

VMEM = functools.partial(pl.BlockSpec, memory_space=pltpu.VMEM)
SMEM = functools.partial(pl.BlockSpec, memory_space=pltpu.SMEM)
HBM = functools.partial(pl.BlockSpec, memory_space=pl.ANY)


def inside(size, shape):
    rows = lax.broadcasted_iota(jnp.int32, shape, 0)
    lanes = lax.broadcasted_iota(jnp.int32, shape, 1)
    return (rows < size) & (lanes < size)


def mask_kernel(size_ref, amplitude_ref, masked_ref):
    for p in range(masked_ref.shape[0]):
        held = inside(size_ref[p], masked_ref.shape[1:])
        value = jnp.where(held, amplitude_ref[p].astype(jnp.float32), 0.0)
        masked_ref[p] = value.astype(masked_ref.dtype)


def base_kernel(size_ref, energy_ref, integral_ref, masked_ref, base_ref):
    shape = base_ref.shape[1:]
    for p in range(base_ref.shape[0]):
        across = jnp.broadcast_to(energy_ref[p : p + 1, :], shape)
        denominator = across.T + across
        value = integral_ref[p].astype(jnp.float32) + denominator * masked_ref[p].astype(jnp.float32)
        base_ref[p] = jnp.where(inside(size_ref[p], shape), value, 0.0)


def list_kernel(
    columns, pairs, me_ref, source_ref, owner_ref, dispatch_ref, result_ref, list_ref, pair_ref
):
    tiles = source_ref.shape[0]
    depth = columns // GROUP
    half = depth // 2
    me = me_ref[0]
    z, g = me // GROUP, me % GROUP

    def fill(i, _):
        list_ref[0, i] = 0
        list_ref[1, i] = 0
        list_ref[2, i] = columns // 2
        return 0

    lax.fori_loop(0, tiles, fill, 0)

    def visit(t, count):
        s, o = source_ref[t], owner_ref[t]
        pair = dispatch_ref[s, me]
        live = (pair >= 0) & (result_ref[me, o] >= 0)

        @pl.when(live)
        def _():
            far = (s // GROUP - z + depth) % depth
            ahead = (o // GROUP - z + depth) % half
            list_ref[0, count] = t
            list_ref[1, count] = (far * GROUP + (g ^ (s % GROUP))) * pairs + jnp.maximum(pair, 0)
            list_ref[2, count] = ahead * GROUP + (g ^ (o % GROUP))

        return count + live.astype(jnp.int32)

    count = lax.fori_loop(0, tiles, visit, jnp.int32(0))
    list_ref[3, 0] = count
    for steps in range(half + 1):
        for m in range(GROUP):
            pair_ref[steps, m] = result_ref[z * GROUP + (g ^ m), (z + steps) % depth * GROUP + g]


def tiles_kernel(list_ref, masked_ref, transfer_ref, block_ref, held, total, arrived):
    count = list_ref[3, 0]
    steps = (count + UNROLL - 1) // UNROLL

    def copy(i):
        return pltpu.make_async_copy(transfer_ref.at[list_ref[0, i]], held.at[i], arrived.at[i])

    def fetch(i, _):
        copy(i).start()
        return 0

    lax.fori_loop(0, steps * UNROLL, fetch, 0)
    total[...] = jnp.zeros_like(total)

    def step(n, _):
        places = [n * UNROLL + u for u in range(UNROLL)]
        for i in places:
            copy(i).wait()
        halves = [
            jnp.dot(held[i], masked_ref[list_ref[1, i]], preferred_element_type=jnp.float32)
            for i in places
        ]
        for i, half in zip(places, halves):
            total[list_ref[2, i]] += lax.dot_general(
                half.astype(jnp.bfloat16),
                held[i],
                (((1,), (1,)), ((), ())),
                preferred_element_type=jnp.float32,
            )
        return 0

    lax.fori_loop(0, steps, step, 0)
    for b in range(block_ref.shape[0]):
        block_ref[b] = total[b].astype(block_ref.dtype)


def shards(
    amplitudes,
    integrals,
    energies,
    pno_size,
    subspace_transfers,
    tile_source,
    tile_owner,
    dispatch_table,
    result_list,
):
    pairs, width = amplitudes.shape[:2]
    tiles = subspace_transfers.shape[0]
    columns = lax.axis_size("col")
    depth = columns // GROUP
    half = depth // 2
    me = lax.axis_index("col").astype(jnp.int32)
    z, g = me // GROUP, me % GROUP

    def swap(value, m):
        return lax.ppermute(value, "col", [(i, i ^ m) for i in range(columns)])

    def ahead(value, steps):
        return lax.ppermute(
            value, "col", [(i, (i + steps * GROUP) % columns) for i in range(columns)]
        )

    masked = pl.pallas_call(
        mask_kernel,
        out_shape=jax.ShapeDtypeStruct(amplitudes.shape, jnp.bfloat16),
        in_specs=[SMEM(), VMEM()],
        out_specs=VMEM(),
        name="mask",
    )(pno_size, amplitudes)

    lane = [masked] + [ahead(masked, -far) for far in range(1, depth)]
    across = [swap(part, 2) for part in lane]
    both = [jnp.stack([a, b]) for a, b in zip(lane, across)]
    other = [swap(part, 1) for part in both]
    everyone = jnp.stack(
        [jnp.stack([a[0], b[0], a[1], b[1]]) for a, b in zip(both, other)]
    ).reshape(columns * pairs, width, width)

    tile_list, fed = pl.pallas_call(
        functools.partial(list_kernel, columns, pairs),
        out_shape=[
            jax.ShapeDtypeStruct((4, tiles), jnp.int32),
            jax.ShapeDtypeStruct((half + 1, GROUP), jnp.int32),
        ],
        in_specs=[SMEM()] * 5,
        out_specs=[SMEM(), SMEM()],
        name="tile_list",
    )(me[None], tile_source, tile_owner, dispatch_table, result_list)

    blocks = pl.pallas_call(
        tiles_kernel,
        out_shape=jax.ShapeDtypeStruct((columns // 2, width, width), jnp.bfloat16),
        in_specs=[SMEM(), VMEM(), HBM()],
        out_specs=VMEM(),
        scratch_shapes=[
            pltpu.VMEM((tiles, width, width), jnp.bfloat16),
            pltpu.VMEM((columns // 2 + 1, width, width), jnp.float32),
            pltpu.SemaphoreType.DMA((tiles,)),
        ],
        compiler_params=pltpu.CompilerParams(vmem_limit_bytes=48 * 2**20),
        cost_estimate=pl.CostEstimate(
            flops=4 * tiles * width**3, bytes_accessed=2 * tiles * width**2, transcendentals=0
        ),
        name="tiles",
    )(tile_list, everyone, subspace_transfers)

    near = (g ^ jnp.arange(GROUP, dtype=jnp.int32)) < g
    stays = jnp.where(near, fed[0], -1)
    onward = jnp.concatenate([jnp.where(near, -1, fed[half])[None], fed[1:half]])
    pair_ids = jnp.arange(pairs, dtype=jnp.int32)

    def by_pair(parts, fed_pairs):
        chosen = (fed_pairs[:, None] == pair_ids)[:, :, None, None]
        terms = [jnp.where(chosen[m], parts[m].astype(jnp.float32), 0.0) for m in range(GROUP)]
        return functools.reduce(jnp.add, terms)

    coupled = []
    for row in range(half):
        block = [blocks[row * GROUP + m] for m in range(GROUP)]
        block = [block[0]] + [swap(block[m], m) for m in range(1, GROUP)]
        sums = by_pair(block, onward[row]).astype(jnp.bfloat16)
        if row == 0:
            coupled.append(by_pair(block, stays))
        coupled.append(ahead(sums, row if row else half))

    base = pl.pallas_call(
        base_kernel,
        out_shape=jax.ShapeDtypeStruct(amplitudes.shape, jnp.float32),
        in_specs=[SMEM(), VMEM(), VMEM(), VMEM()],
        out_specs=VMEM(),
        name="base",
    )(pno_size, energies, integrals, masked)

    total = functools.reduce(jnp.add, [part.astype(jnp.float32) for part in coupled], base)
    lanes = jnp.arange(width, dtype=jnp.int32)
    held = lanes[None, :] < pno_size[:, None]
    return jnp.where(held[:, :, None] & held[:, None, :], total, 0.0)


def solution(mesh):
    placed = (
        P(("frag", "col"), None, None),
        P(("frag", "col"), None, None),
        P(("frag", "col"), None),
        P(("frag", "col")),
        P(("frag", "col"), None, None),
        P(("frag", "col")),
        P(("frag", "col")),
        P("frag", None),
        P("frag", None),
    )
    return jax.shard_map(
        shards,
        mesh=mesh,
        in_specs=placed,
        out_specs=P(("frag", "col"), None, None),
        check_vma=False,
    )
```

```python
import functools

import jax
import jax.numpy as jnp
from jax import lax
from jax.experimental import pallas as pl
from jax.experimental.pallas import tpu as pltpu
from jax.sharding import PartitionSpec as P

GROUP = 4
UNROLL = 8

VMEM = functools.partial(pl.BlockSpec, memory_space=pltpu.VMEM)
SMEM = functools.partial(pl.BlockSpec, memory_space=pltpu.SMEM)
HBM = functools.partial(pl.BlockSpec, memory_space=pl.ANY)


def inside(size, shape):
    rows = lax.broadcasted_iota(jnp.int32, shape, 0)
    lanes = lax.broadcasted_iota(jnp.int32, shape, 1)
    return (rows < size) & (lanes < size)


def mask_kernel(size_ref, amplitude_ref, masked_ref):
    for p in range(masked_ref.shape[0]):
        held = inside(size_ref[p], masked_ref.shape[1:])
        value = jnp.where(held, amplitude_ref[p].astype(jnp.float32), 0.0)
        masked_ref[p] = value.astype(masked_ref.dtype)


def base_kernel(size_ref, energy_ref, integral_ref, masked_ref, base_ref):
    shape = base_ref.shape[1:]
    for p in range(base_ref.shape[0]):
        across = jnp.broadcast_to(energy_ref[p : p + 1, :], shape)
        denominator = across.T + across
        value = integral_ref[p].astype(jnp.float32) + denominator * masked_ref[p].astype(jnp.float32)
        base_ref[p] = jnp.where(inside(size_ref[p], shape), value, 0.0)


def list_kernel(
    columns, pairs, me_ref, source_ref, owner_ref, dispatch_ref, result_ref, list_ref, pair_ref
):
    tiles = source_ref.shape[0]
    depth = columns // GROUP
    half = depth // 2
    me = me_ref[0]
    z, g = me // GROUP, me % GROUP

    def visit(t, counts):
        s, o = source_ref[t], owner_ref[t]
        pair = dispatch_ref[s, me]
        live = (pair >= 0) & (result_ref[me, o] >= 0)
        row = (o // GROUP - z + depth) % half
        later = (row > 0).astype(jnp.int32)
        count = jnp.where(row > 0, counts[1], counts[0])

        @pl.when(live)
        def _():
            list_ref[later, 0, count] = t
            list_ref[later, 1, count] = (me ^ s) * pairs + jnp.maximum(pair, 0)
            list_ref[later, 2, count] = (row - later) * GROUP + (g ^ (o % GROUP))

        one = live.astype(jnp.int32)
        return counts[0] + one * (1 - later), counts[1] + one * later

    counts = lax.fori_loop(0, tiles, visit, (jnp.int32(0), jnp.int32(0)))
    for part in range(2):
        count = counts[part]
        spare = GROUP * (half - 1 if part else 1)

        def fill(i, _):
            list_ref[part, 0, i] = 0
            list_ref[part, 1, i] = 0
            list_ref[part, 2, i] = spare
            return 0

        lax.fori_loop(count, (count + UNROLL - 1) // UNROLL * UNROLL, fill, 0)
        list_ref[part, 3, 0] = count
    for steps in range(half + 1):
        for m in range(GROUP):
            pair_ref[steps, m] = result_ref[z * GROUP + (g ^ m), (z + steps) % depth * GROUP + g]


def tiles_kernel(part, list_ref, masked_ref, transfer_ref, *refs):
    block_ref, total = refs[-2:]
    steps = (list_ref[part, 3, 0] + UNROLL - 1) // UNROLL
    total[...] = jnp.zeros_like(total)

    def step(n, _):
        places = [n * UNROLL + u for u in range(UNROLL)]
        tiles = [list_ref[part, 0, i] for i in places]
        halves = [
            jnp.dot(
                transfer_ref[t],
                masked_ref[list_ref[part, 1, i]],
                preferred_element_type=jnp.float32,
            )
            for i, t in zip(places, tiles)
        ]
        for i, t, half in zip(places, tiles, halves):
            total[list_ref[part, 2, i]] += lax.dot_general(
                half.astype(jnp.bfloat16),
                transfer_ref[t],
                (((1,), (1,)), ((), ())),
                preferred_element_type=jnp.float32,
            )
        return 0

    lax.fori_loop(0, steps, step, 0)
    for b in range(block_ref.shape[0]):
        block_ref[b] = total[b].astype(block_ref.dtype)


def shards(
    amplitudes,
    integrals,
    energies,
    pno_size,
    subspace_transfers,
    tile_source,
    tile_owner,
    dispatch_table,
    result_list,
):
    pairs, width = amplitudes.shape[:2]
    tiles = subspace_transfers.shape[0]
    columns = lax.axis_size("col")
    depth = columns // GROUP
    half = depth // 2
    me = lax.axis_index("col").astype(jnp.int32)
    z, g = me // GROUP, me % GROUP

    def swap(value, m):
        return lax.ppermute(value, "col", [(i, i ^ m) for i in range(columns)])

    def ahead(value, steps):
        return lax.ppermute(
            value, "col", [(i, (i + steps * GROUP) % columns) for i in range(columns)]
        )

    masked = pl.pallas_call(
        mask_kernel,
        out_shape=jax.ShapeDtypeStruct(amplitudes.shape, jnp.bfloat16),
        in_specs=[SMEM(), VMEM()],
        out_specs=VMEM(),
        name="mask",
    )(pno_size, amplitudes)

    lane, across = [masked] + [None] * (depth - 1), [None] * depth
    for x in range(1, depth, 2):
        lane[x] = swap(masked, x * GROUP)
        across[x - 1 if x == 1 else x] = swap(lane[x - 1 if x == 1 else x], 2)
    across[1] = swap(lane[1], 2)
    for x in range(2, depth, 2):
        lane[x] = swap(lane[x + 1], GROUP)
        across[x] = jnp.concatenate(
            [swap(lane[x][: pairs // 2], 2), swap(across[x + 1][pairs // 2 :], GROUP)]
        )
    everyone = []
    for x in range(depth):
        everyone += [lane[x], swap(lane[x], 1), across[x], swap(across[x], 1)]
    everyone = jnp.concatenate(everyone)

    tile_list, fed = pl.pallas_call(
        functools.partial(list_kernel, columns, pairs),
        out_shape=[
            jax.ShapeDtypeStruct((2, 4, tiles + UNROLL), jnp.int32),
            jax.ShapeDtypeStruct((half + 1, GROUP), jnp.int32),
        ],
        in_specs=[SMEM()] * 5,
        out_specs=[SMEM(), SMEM()],
        name="tile_list",
    )(me[None], tile_source, tile_owner, dispatch_table, result_list)

    def sums_of(part, rows, *after):
        return pl.pallas_call(
            functools.partial(tiles_kernel, part),
            out_shape=jax.ShapeDtypeStruct((rows * GROUP, width, width), jnp.bfloat16),
            in_specs=[SMEM(), VMEM(), VMEM()] + [HBM()] * len(after),
            out_specs=VMEM(),
            scratch_shapes=[pltpu.VMEM((rows * GROUP + 1, width, width), jnp.float32)],
            compiler_params=pltpu.CompilerParams(vmem_limit_bytes=16 * 2**20),
            cost_estimate=pl.CostEstimate(
                flops=2 * tiles * width**3, bytes_accessed=tiles * width**2, transcendentals=0
            ),
            name="tiles",
        )(tile_list, everyone, subspace_transfers, *after)

    def spread(block):
        return [block[0]] + [swap(block[m], m) for m in range(1, GROUP)]

    first = spread(sums_of(0, 1))
    others = sums_of(1, half - 1, first[1])
    rows = [first] + [spread(others[i * GROUP : (i + 1) * GROUP]) for i in range(half - 1)]

    near = (g ^ jnp.arange(GROUP, dtype=jnp.int32)) < g
    stays = jnp.where(near, fed[0], -1)
    onward = jnp.concatenate([jnp.where(near, -1, fed[half])[None], fed[1:half]])
    pair_ids = jnp.arange(pairs, dtype=jnp.int32)

    def by_pair(parts, fed_pairs):
        chosen = (fed_pairs[:, None] == pair_ids)[:, :, None, None]
        terms = [jnp.where(chosen[m], parts[m].astype(jnp.float32), 0.0) for m in range(GROUP)]
        return functools.reduce(jnp.add, terms)

    coupled = []
    for row, block in enumerate(rows):
        sums = by_pair(block, onward[row]).astype(jnp.bfloat16)
        if row == 0:
            coupled.append(by_pair(block, stays))
        coupled.append(ahead(sums, row if row else half))

    base = pl.pallas_call(
        base_kernel,
        out_shape=jax.ShapeDtypeStruct(amplitudes.shape, jnp.float32),
        in_specs=[SMEM(), VMEM(), VMEM(), VMEM()],
        out_specs=VMEM(),
        name="base",
    )(pno_size, energies, integrals, masked)

    total = functools.reduce(jnp.add, [part.astype(jnp.float32) for part in coupled], base)
    lanes = jnp.arange(width, dtype=jnp.int32)
    held = lanes[None, :] < pno_size[:, None]
    return jnp.where(held[:, :, None] & held[:, None, :], total, 0.0)


def solution(mesh):
    placed = (
        P(("frag", "col"), None, None),
        P(("frag", "col"), None, None),
        P(("frag", "col"), None),
        P(("frag", "col")),
        P(("frag", "col"), None, None),
        P(("frag", "col")),
        P(("frag", "col")),
        P("frag", None),
        P("frag", None),
    )
    return jax.shard_map(
        shards,
        mesh=mesh,
        in_specs=placed,
        out_specs=P(("frag", "col"), None, None),
        check_vma=False,
    )
```

```python
import functools

import jax
import jax.numpy as jnp
from jax import lax
from jax.experimental import pallas as pl
from jax.experimental.pallas import tpu as pltpu
from jax.sharding import PartitionSpec as P

GROUP = 4
UNROLL = 8

VMEM = functools.partial(pl.BlockSpec, memory_space=pltpu.VMEM)
SMEM = functools.partial(pl.BlockSpec, memory_space=pltpu.SMEM)
HBM = functools.partial(pl.BlockSpec, memory_space=pl.ANY)


def inside(size, shape):
    rows = lax.broadcasted_iota(jnp.int32, shape, 0)
    lanes = lax.broadcasted_iota(jnp.int32, shape, 1)
    return (rows < size) & (lanes < size)


def mask_kernel(size_ref, amplitude_ref, masked_ref):
    for p in range(masked_ref.shape[0]):
        held = inside(size_ref[p], masked_ref.shape[1:])
        value = jnp.where(held, amplitude_ref[p].astype(jnp.float32), 0.0)
        masked_ref[p] = value.astype(masked_ref.dtype)


def base_kernel(size_ref, energy_ref, integral_ref, masked_ref, base_ref):
    shape = base_ref.shape[1:]
    for p in range(base_ref.shape[0]):
        across = jnp.broadcast_to(energy_ref[p : p + 1, :], shape)
        denominator = across.T + across
        value = integral_ref[p].astype(jnp.float32) + denominator * masked_ref[p].astype(jnp.float32)
        base_ref[p] = jnp.where(inside(size_ref[p], shape), value, 0.0)


def list_kernel(
    columns, me_ref, place_ref, source_ref, owner_ref, dispatch_ref, result_ref, list_ref, pair_ref
):
    tiles = source_ref.shape[0]
    depth = columns // GROUP
    half = depth // 2
    me = me_ref[0]
    z, g = me // GROUP, me % GROUP

    def visit(t, counts):
        s, o = source_ref[t], owner_ref[t]
        pair = dispatch_ref[s, me]
        live = (pair >= 0) & (result_ref[me, o] >= 0)
        row = (o // GROUP - z + depth) % half
        later = (row > 0).astype(jnp.int32)
        count = jnp.where(row > 0, counts[1], counts[0])

        @pl.when(live)
        def _():
            list_ref[later, 0, count] = t
            list_ref[later, 1, count] = place_ref[me ^ s] + jnp.maximum(pair, 0)
            list_ref[later, 2, count] = (row - later) * GROUP + (g ^ (o % GROUP))

        one = live.astype(jnp.int32)
        return counts[0] + one * (1 - later), counts[1] + one * later

    counts = lax.fori_loop(0, tiles, visit, (jnp.int32(0), jnp.int32(0)))
    for part in range(2):
        count = counts[part]
        spare = GROUP * (half - 1 if part else 1)

        def fill(i, _):
            list_ref[part, 0, i] = 0
            list_ref[part, 1, i] = 0
            list_ref[part, 2, i] = spare
            return 0

        lax.fori_loop(count, (count + UNROLL - 1) // UNROLL * UNROLL, fill, 0)
        list_ref[part, 3, 0] = count
    for steps in range(half + 1):
        for m in range(GROUP):
            pair_ref[steps, m] = result_ref[z * GROUP + (g ^ m), (z + steps) % depth * GROUP + g]


def tiles_kernel(part, list_ref, masked_ref, transfer_ref, *refs):
    block_ref, total = refs[-2:]
    steps = (list_ref[part, 3, 0] + UNROLL - 1) // UNROLL
    total[...] = jnp.zeros_like(total)

    def step(n, _):
        places = [n * UNROLL + u for u in range(UNROLL)]
        tiles = [list_ref[part, 0, i] for i in places]
        halves = [
            jnp.dot(
                transfer_ref[t],
                masked_ref[list_ref[part, 1, i]],
                preferred_element_type=jnp.float32,
            )
            for i, t in zip(places, tiles)
        ]
        for i, t, half in zip(places, tiles, halves):
            total[list_ref[part, 2, i]] += lax.dot_general(
                half.astype(jnp.bfloat16),
                transfer_ref[t],
                (((1,), (1,)), ((), ())),
                preferred_element_type=jnp.float32,
            )
        return 0

    lax.fori_loop(0, steps, step, 0)
    for b in range(block_ref.shape[0]):
        block_ref[b] = total[b].astype(block_ref.dtype)


def shards(
    amplitudes,
    integrals,
    energies,
    pno_size,
    subspace_transfers,
    tile_source,
    tile_owner,
    dispatch_table,
    result_list,
):
    pairs, width = amplitudes.shape[:2]
    tiles = subspace_transfers.shape[0]
    columns = lax.axis_size("col")
    depth = columns // GROUP
    half = depth // 2
    me = lax.axis_index("col").astype(jnp.int32)
    z, g = me // GROUP, me % GROUP

    def swap(value, m):
        return lax.ppermute(value, "col", [(i, i ^ m) for i in range(columns)])

    def ahead(value, steps):
        return lax.ppermute(
            value, "col", [(i, (i + steps * GROUP) % columns) for i in range(columns)]
        )

    masked = pl.pallas_call(
        mask_kernel,
        out_shape=jax.ShapeDtypeStruct(amplitudes.shape, jnp.bfloat16),
        in_specs=[SMEM(), VMEM()],
        out_specs=VMEM(),
        name="mask",
    )(pno_size, amplitudes)

    odd, even = list(range(depth - 1, 0, -2)), list(range(2, depth, 2))
    lane = {x: swap(masked, x * GROUP) for x in odd} | {0: masked}
    lane |= {x: swap(lane[x + 1], GROUP) for x in even}
    across = {x: swap(lane[x], 2) for x in [0] + odd}
    across |= {
        x: jnp.concatenate(
            [swap(lane[x][: pairs // 2], 2), swap(across[x + 1][pairs // 2 :], GROUP)]
        )
        for x in even
    }
    held, places = [], []
    for x in odd + [0] + even:
        for m, part in ((x * GROUP, lane[x]), (x * GROUP + 2, across[x])):
            held += [part, swap(part, 1)]
            places += [m, m ^ 1]
    everyone = jnp.concatenate(held)
    place = jnp.array([places.index(m) * pairs for m in range(columns)], jnp.int32)

    tile_list, fed = pl.pallas_call(
        functools.partial(list_kernel, columns),
        out_shape=[
            jax.ShapeDtypeStruct((2, 4, tiles + UNROLL), jnp.int32),
            jax.ShapeDtypeStruct((half + 1, GROUP), jnp.int32),
        ],
        in_specs=[SMEM()] * 6,
        out_specs=[SMEM(), SMEM()],
        name="tile_list",
    )(me[None], place, tile_source, tile_owner, dispatch_table, result_list)

    def sums_of(part, rows, *after):
        return pl.pallas_call(
            functools.partial(tiles_kernel, part),
            out_shape=jax.ShapeDtypeStruct((rows * GROUP, width, width), jnp.bfloat16),
            in_specs=[SMEM(), VMEM(), VMEM()] + [HBM()] * len(after),
            out_specs=VMEM(),
            scratch_shapes=[pltpu.VMEM((rows * GROUP + 1, width, width), jnp.float32)],
            compiler_params=pltpu.CompilerParams(vmem_limit_bytes=16 * 2**20),
            cost_estimate=pl.CostEstimate(
                flops=2 * tiles * width**3, bytes_accessed=tiles * width**2, transcendentals=0
            ),
            name="tiles",
        )(tile_list, everyone, subspace_transfers, *after)

    def spread(block):
        return [block[0]] + [swap(block[m], m) for m in range(1, GROUP)]

    first = spread(sums_of(0, 1))
    others = sums_of(1, half - 1, first[1])
    rows = [first] + [spread(others[i * GROUP : (i + 1) * GROUP]) for i in range(half - 1)]

    near = (g ^ jnp.arange(GROUP, dtype=jnp.int32)) < g
    stays = jnp.where(near, fed[0], -1)
    onward = jnp.concatenate([jnp.where(near, -1, fed[half])[None], fed[1:half]])
    pair_ids = jnp.arange(pairs, dtype=jnp.int32)

    def by_pair(parts, fed_pairs):
        chosen = (fed_pairs[:, None] == pair_ids)[:, :, None, None]
        terms = [jnp.where(chosen[m], parts[m].astype(jnp.float32), 0.0) for m in range(GROUP)]
        return functools.reduce(jnp.add, terms)

    coupled = []
    for row, block in enumerate(rows):
        sums = by_pair(block, onward[row]).astype(jnp.bfloat16)
        if row == 0:
            coupled.append(by_pair(block, stays))
        coupled.append(ahead(sums, row if row else half))

    base = pl.pallas_call(
        base_kernel,
        out_shape=jax.ShapeDtypeStruct(amplitudes.shape, jnp.float32),
        in_specs=[SMEM(), VMEM(), VMEM(), VMEM()],
        out_specs=VMEM(),
        name="base",
    )(pno_size, energies, integrals, masked)

    total = functools.reduce(jnp.add, [part.astype(jnp.float32) for part in coupled], base)
    lanes = jnp.arange(width, dtype=jnp.int32)
    live = lanes[None, :] < pno_size[:, None]
    return jnp.where(live[:, :, None] & live[:, None, :], total, 0.0)


def solution(mesh):
    placed = (
        P(("frag", "col"), None, None),
        P(("frag", "col"), None, None),
        P(("frag", "col"), None),
        P(("frag", "col")),
        P(("frag", "col"), None, None),
        P(("frag", "col")),
        P(("frag", "col")),
        P("frag", None),
        P("frag", None),
    )
    return jax.shard_map(
        shards,
        mesh=mesh,
        in_specs=placed,
        out_specs=P(("frag", "col"), None, None),
        check_vma=False,
    )
```

```python
import functools

import jax
import jax.numpy as jnp
from jax import lax
from jax.experimental import pallas as pl
from jax.experimental.pallas import tpu as pltpu
from jax.sharding import PartitionSpec as P

GROUP = 4
UNROLL = 8

VMEM = functools.partial(pl.BlockSpec, memory_space=pltpu.VMEM)
SMEM = functools.partial(pl.BlockSpec, memory_space=pltpu.SMEM)
HBM = functools.partial(pl.BlockSpec, memory_space=pl.ANY)


def inside(size, shape):
    rows = lax.broadcasted_iota(jnp.int32, shape, 0)
    lanes = lax.broadcasted_iota(jnp.int32, shape, 1)
    return (rows < size) & (lanes < size)


def mask_kernel(size_ref, amplitude_ref, masked_ref):
    for p in range(masked_ref.shape[0]):
        held = inside(size_ref[p], masked_ref.shape[1:])
        value = jnp.where(held, amplitude_ref[p].astype(jnp.float32), 0.0)
        masked_ref[p] = value.astype(masked_ref.dtype)


def base_kernel(size_ref, energy_ref, integral_ref, masked_ref, base_ref):
    shape = base_ref.shape[1:]
    for p in range(base_ref.shape[0]):
        across = jnp.broadcast_to(energy_ref[p : p + 1, :], shape)
        denominator = across.T + across
        value = integral_ref[p].astype(jnp.float32) + denominator * masked_ref[p].astype(jnp.float32)
        base_ref[p] = jnp.where(inside(size_ref[p], shape), value, 0.0)


def list_kernel(
    columns, early, me_ref, place_ref, source_ref, owner_ref, dispatch_ref, result_ref, transfer_ref, list_ref, pair_ref, held_ref, arrived
):
    tiles = source_ref.shape[0]
    depth = columns // GROUP
    half = depth // 2
    me = me_ref[0]
    fetch = pltpu.make_async_copy(transfer_ref, held_ref, arrived)
    fetch.start()
    z, g = me // GROUP, me % GROUP

    def visit(t, counts):
        s, o = source_ref[t], owner_ref[t]
        pair = dispatch_ref[s, me]
        live = (pair >= 0) & (result_ref[me, o] >= 0)
        where = place_ref[me ^ s]
        row = (o // GROUP - z + depth) % half
        part = jnp.where(where < early, 0, jnp.where(row == 0, 1, 2))
        count = jnp.where(part == 0, counts[0], jnp.where(part == 1, counts[1], counts[2]))

        @pl.when(live)
        def _():
            list_ref[part, 0, count] = t
            list_ref[part, 1, count] = jnp.where(part == 0, where, where - early) + jnp.maximum(pair, 0)
            list_ref[part, 2, count] = (row - part // 2) * GROUP + (g ^ (o % GROUP))

        one = live.astype(jnp.int32)
        return tuple(n + one * (part == p).astype(jnp.int32) for p, n in enumerate(counts))

    counts = lax.fori_loop(0, tiles, visit, (jnp.int32(0),) * 3)
    for part, rows in enumerate((half, 1, half - 1)):
        count = counts[part]
        spare = GROUP * rows

        def fill(i, _):
            list_ref[part, 0, i] = 0
            list_ref[part, 1, i] = 0
            list_ref[part, 2, i] = spare
            return 0

        lax.fori_loop(count, (count + UNROLL - 1) // UNROLL * UNROLL, fill, 0)
        list_ref[part, 3, 0] = count
    for steps in range(half + 1):
        for m in range(GROUP):
            pair_ref[steps, m] = result_ref[z * GROUP + (g ^ m), (z + steps) % depth * GROUP + g]
    fetch.wait()


def add_tiles(part, list_ref, masked_ref, transfer_ref, total):
    def step(n, _):
        places = [n * UNROLL + u for u in range(UNROLL)]
        tiles = [list_ref[part, 0, i] for i in places]
        halves = [
            jnp.dot(
                transfer_ref[t],
                masked_ref[list_ref[part, 1, i]],
                preferred_element_type=jnp.float32,
            )
            for i, t in zip(places, tiles)
        ]
        for i, t, half in zip(places, tiles, halves):
            total[list_ref[part, 2, i]] += lax.dot_general(
                half.astype(jnp.bfloat16),
                transfer_ref[t],
                (((1,), (1,)), ((), ())),
                preferred_element_type=jnp.float32,
            )
        return 0

    lax.fori_loop(0, (list_ref[part, 3, 0] + UNROLL - 1) // UNROLL, step, 0)


def early_kernel(list_ref, masked_ref, transfer_ref, total):
    total[...] = jnp.zeros_like(total)
    add_tiles(0, list_ref, masked_ref, transfer_ref, total)


def late_kernel(part, list_ref, masked_ref, transfer_ref, sum_ref, *refs):
    block_ref, total = refs[-2:]
    blocks = block_ref.shape[0]
    total[:blocks] = sum_ref[pl.ds(GROUP * (part - 1), blocks)]
    add_tiles(part, list_ref, masked_ref, transfer_ref, total)
    for b in range(blocks):
        block_ref[b] = total[b].astype(block_ref.dtype)


def shards(
    amplitudes,
    integrals,
    energies,
    pno_size,
    subspace_transfers,
    tile_source,
    tile_owner,
    dispatch_table,
    result_list,
):
    pairs, width = amplitudes.shape[:2]
    tiles = subspace_transfers.shape[0]
    columns = lax.axis_size("col")
    depth = columns // GROUP
    half = depth // 2
    me = lax.axis_index("col").astype(jnp.int32)
    z, g = me // GROUP, me % GROUP

    def swap(value, m):
        return lax.ppermute(value, "col", [(i, i ^ m) for i in range(columns)])

    def ahead(value, steps):
        return lax.ppermute(
            value, "col", [(i, (i + steps * GROUP) % columns) for i in range(columns)]
        )

    masked = pl.pallas_call(
        mask_kernel,
        out_shape=pltpu.VMEM(amplitudes.shape, jnp.bfloat16),
        in_specs=[SMEM(), VMEM()],
        out_specs=VMEM(),
        name="mask",
    )(pno_size, amplitudes)

    odd, even = list(range(depth - 1, 0, -2)), list(range(2, depth, 2))
    lane = {x: swap(masked, x * GROUP) for x in odd} | {0: masked}
    lane |= {x: swap(lane[x + 1], GROUP) for x in even}
    across = {x: swap(lane[x], 2) for x in [0] + odd}

    def with_other(parts):
        held = [value for part in parts.values() for value in (part, swap(part, 1))]
        return jnp.concatenate(held), [n for m in parts for n in (m, m ^ 1)]

    own = {x * GROUP: lane[x] for x in odd + [0]} | {2: across[0]}
    early, places = with_other(own)
    later = [x * GROUP + 2 for x in odd] + [x * GROUP + y for x in even for y in (0, 2)]
    order = places + [n for m in later for n in (m, m ^ 1)]
    place = jnp.array([order.index(m) * pairs for m in range(columns)], jnp.int32)

    in_hbm = [
        pltpu.with_memory_space_constraint(value, pltpu.HBM)
        for value in (tile_source, tile_owner, dispatch_table, result_list, subspace_transfers)
    ]
    tile_list, fed, transfers = pl.pallas_call(
        functools.partial(list_kernel, columns, len(places) * pairs),
        out_shape=[
            jax.ShapeDtypeStruct((3, 4, tiles + UNROLL), jnp.int32),
            jax.ShapeDtypeStruct((half + 1, GROUP), jnp.int32),
            pltpu.VMEM(subspace_transfers.shape, jnp.bfloat16),
        ],
        in_specs=[SMEM()] * 6 + [HBM()],
        out_specs=[SMEM(), SMEM(), VMEM()],
        scratch_shapes=[pltpu.SemaphoreType.DMA],
        compiler_params=pltpu.CompilerParams(vmem_limit_bytes=16 * 2**20),
        name="tile_list",
    )(me[None], place, *in_hbm)

    work = pl.CostEstimate(
        flops=2 * tiles * width**3, bytes_accessed=tiles * width**2, transcendentals=0
    )
    totals = pl.pallas_call(
        early_kernel,
        out_shape=jax.ShapeDtypeStruct((columns // 2 + 1, width, width), jnp.float32),
        in_specs=[SMEM(), VMEM(), VMEM()],
        out_specs=VMEM(),
        compiler_params=pltpu.CompilerParams(vmem_limit_bytes=16 * 2**20),
        cost_estimate=work,
        name="early_tiles",
    )(tile_list, early, transfers)

    for x in even:
        lane[x], totals = lax.optimization_barrier((lane[x], totals))
        across[x] = jnp.concatenate(
            [swap(lane[x][: pairs // 2], 2), swap(across[x + 1][pairs // 2 :], GROUP)]
        )
    parts = {x * GROUP + 2: across[x] for x in odd}
    parts |= {x * GROUP + y: part[x] for x in even for y, part in ((0, lane), (2, across))}
    late, _ = with_other(parts)

    def sums_of(part, rows, *after):
        return pl.pallas_call(
            functools.partial(late_kernel, part),
            out_shape=jax.ShapeDtypeStruct((rows * GROUP, width, width), jnp.bfloat16),
            in_specs=[SMEM(), VMEM(), VMEM(), VMEM()] + [HBM()] * len(after),
            out_specs=VMEM(),
            scratch_shapes=[pltpu.VMEM((rows * GROUP + 1, width, width), jnp.float32)],
            compiler_params=pltpu.CompilerParams(vmem_limit_bytes=16 * 2**20),
            cost_estimate=work,
            name="late_tiles",
        )(tile_list, late, transfers, totals, *after)

    def spread(block):
        return [block[0]] + [swap(block[m], m) for m in range(1, GROUP)]

    first = spread(sums_of(1, 1))
    others = sums_of(2, half - 1, first[1])
    rows = [first] + [spread(others[i * GROUP : (i + 1) * GROUP]) for i in range(half - 1)]

    near = (g ^ jnp.arange(GROUP, dtype=jnp.int32)) < g
    stays = jnp.where(near, fed[0], -1)
    onward = jnp.concatenate([jnp.where(near, -1, fed[half])[None], fed[1:half]])
    pair_ids = jnp.arange(pairs, dtype=jnp.int32)

    def by_pair(parts, fed_pairs):
        chosen = (fed_pairs[:, None] == pair_ids)[:, :, None, None]
        terms = [jnp.where(chosen[m], parts[m].astype(jnp.float32), 0.0) for m in range(GROUP)]
        return functools.reduce(jnp.add, terms)

    coupled = []
    for row, block in enumerate(rows):
        sums = by_pair(block, onward[row]).astype(jnp.bfloat16)
        if row == 0:
            coupled.append(by_pair(block, stays))
        coupled.append(ahead(sums, row if row else half))

    base = pl.pallas_call(
        base_kernel,
        out_shape=pltpu.VMEM(amplitudes.shape, jnp.float32),
        in_specs=[SMEM(), VMEM(), VMEM(), VMEM()],
        out_specs=VMEM(),
        name="base",
    )(pno_size, energies, integrals, masked)

    total = functools.reduce(jnp.add, [part.astype(jnp.float32) for part in coupled], base)
    lanes = jnp.arange(width, dtype=jnp.int32)
    live = lanes[None, :] < pno_size[:, None]
    return jnp.where(live[:, :, None] & live[:, None, :], total, 0.0)


def solution(mesh):
    placed = (
        P(("frag", "col"), None, None),
        P(("frag", "col"), None, None),
        P(("frag", "col"), None),
        P(("frag", "col")),
        P(("frag", "col"), None, None),
        P(("frag", "col")),
        P(("frag", "col")),
        P("frag", None),
        P("frag", None),
    )
    return jax.shard_map(
        shards,
        mesh=mesh,
        in_specs=placed,
        out_specs=P(("frag", "col"), None, None),
        check_vma=False,
    )
```

```python
import functools

import jax
import jax.numpy as jnp
from jax import lax
from jax.experimental import pallas as pl
from jax.experimental.pallas import tpu as pltpu
from jax.sharding import PartitionSpec as P

GROUP = 4
UNROLL = 10

VMEM = functools.partial(pl.BlockSpec, memory_space=pltpu.VMEM)
SMEM = functools.partial(pl.BlockSpec, memory_space=pltpu.SMEM)
HBM = functools.partial(pl.BlockSpec, memory_space=pl.ANY)


def inside(size, shape):
    rows = lax.broadcasted_iota(jnp.int32, shape, 0)
    lanes = lax.broadcasted_iota(jnp.int32, shape, 1)
    return (rows < size) & (lanes < size)


def mask_kernel(size_ref, amplitude_ref, masked_ref):
    for p in range(masked_ref.shape[0]):
        held = inside(size_ref[p], masked_ref.shape[1:])
        value = jnp.where(held, amplitude_ref[p].astype(jnp.float32), 0.0)
        masked_ref[p] = value.astype(masked_ref.dtype)


def base_kernel(size_ref, energy_ref, integral_ref, masked_ref, base_ref):
    shape = base_ref.shape[1:]
    for p in range(base_ref.shape[0]):
        across = jnp.broadcast_to(energy_ref[p : p + 1, :], shape)
        denominator = across.T + across
        value = integral_ref[p].astype(jnp.float32) + denominator * masked_ref[p].astype(jnp.float32)
        base_ref[p] = jnp.where(inside(size_ref[p], shape), value, 0.0)


def list_kernel(
    columns, early, me_ref, place_ref, source_ref, owner_ref, dispatch_ref, result_ref, transfer_ref, list_ref, pair_ref, held_ref, arrived
):
    tiles = source_ref.shape[0]
    depth = columns // GROUP
    half = depth // 2
    me = me_ref[0]
    fetch = pltpu.make_async_copy(transfer_ref, held_ref, arrived)
    fetch.start()
    z, g = me // GROUP, me % GROUP

    def visit(t, counts):
        s, o = source_ref[t], owner_ref[t]
        pair = dispatch_ref[s, me]
        live = (pair >= 0) & (result_ref[me, o] >= 0)
        where = place_ref[me ^ s]
        row = (o // GROUP - z + depth) % half
        part = jnp.where(where < early, 0, jnp.where(row == 0, 1, 2))
        count = jnp.where(part == 0, counts[0], jnp.where(part == 1, counts[1], counts[2]))

        @pl.when(live)
        def _():
            list_ref[part, 0, count] = t
            list_ref[part, 1, count] = jnp.where(part == 0, where, where - early) + jnp.maximum(pair, 0)
            list_ref[part, 2, count] = (row - part // 2) * GROUP + (g ^ (o % GROUP))

        one = live.astype(jnp.int32)
        return tuple(n + one * (part == p).astype(jnp.int32) for p, n in enumerate(counts))

    counts = lax.fori_loop(0, tiles, visit, (jnp.int32(0),) * 3)
    for part, rows in enumerate((half, 1, half - 1)):
        count = counts[part]
        spare = GROUP * rows

        def fill(i, _):
            list_ref[part, 0, i] = 0
            list_ref[part, 1, i] = 0
            list_ref[part, 2, i] = spare
            return 0

        lax.fori_loop(count, (count + UNROLL - 1) // UNROLL * UNROLL, fill, 0)
        list_ref[part, 3, 0] = count
    for steps in range(half + 1):
        for m in range(GROUP):
            pair_ref[steps, m] = result_ref[z * GROUP + (g ^ m), (z + steps) % depth * GROUP + g]
    fetch.wait()


def add_tiles(part, list_ref, masked_ref, transfer_ref, total):
    def step(n, _):
        places = [n * UNROLL + u for u in range(UNROLL)]
        tiles = [list_ref[part, 0, i] for i in places]
        halves = [
            jnp.dot(
                transfer_ref[t],
                masked_ref[list_ref[part, 1, i]],
                preferred_element_type=jnp.float32,
            )
            for i, t in zip(places, tiles)
        ]
        for i, t, half in zip(places, tiles, halves):
            total[list_ref[part, 2, i]] += lax.dot_general(
                half.astype(jnp.bfloat16),
                transfer_ref[t],
                (((1,), (1,)), ((), ())),
                preferred_element_type=jnp.float32,
            )
        return 0

    lax.fori_loop(0, (list_ref[part, 3, 0] + UNROLL - 1) // UNROLL, step, 0)


def early_kernel(list_ref, masked_ref, transfer_ref, total):
    total[...] = jnp.zeros_like(total)
    add_tiles(0, list_ref, masked_ref, transfer_ref, total)


def late_kernel(part, list_ref, masked_ref, transfer_ref, sum_ref, *refs):
    block_ref, total = refs[-2:]
    blocks = block_ref.shape[0]
    total[:blocks] = sum_ref[pl.ds(GROUP * (part - 1), blocks)]
    add_tiles(part, list_ref, masked_ref, transfer_ref, total)
    for b in range(blocks):
        block_ref[b] = total[b].astype(block_ref.dtype)


def shards(
    amplitudes,
    integrals,
    energies,
    pno_size,
    subspace_transfers,
    tile_source,
    tile_owner,
    dispatch_table,
    result_list,
):
    pairs, width = amplitudes.shape[:2]
    tiles = subspace_transfers.shape[0]
    columns = lax.axis_size("col")
    depth = columns // GROUP
    half = depth // 2
    me = lax.axis_index("col").astype(jnp.int32)
    z, g = me // GROUP, me % GROUP

    def swap(value, m):
        return lax.ppermute(value, "col", [(i, i ^ m) for i in range(columns)])

    def ahead(value, steps):
        return lax.ppermute(
            value, "col", [(i, (i + steps * GROUP) % columns) for i in range(columns)]
        )

    masked = pl.pallas_call(
        mask_kernel,
        out_shape=pltpu.VMEM(amplitudes.shape, jnp.bfloat16),
        in_specs=[SMEM(), VMEM()],
        out_specs=VMEM(),
        name="mask",
    )(pno_size, amplitudes)

    odd, even = list(range(depth - 1, 0, -2)), list(range(2, depth, 2))
    lane = {x: swap(masked, x * GROUP) for x in odd} | {0: masked}
    lane |= {x: swap(lane[x + 1], GROUP) for x in even}
    across = {x: swap(lane[x], 2) for x in [0] + odd}

    def with_other(parts):
        held = [value for part in parts.values() for value in (part, swap(part, 1))]
        return jnp.concatenate(held), [n for m in parts for n in (m, m ^ 1)]

    own = {x * GROUP: lane[x] for x in odd + [0]} | {2: across[0]}
    early, places = with_other(own)
    later = [x * GROUP + 2 for x in odd] + [x * GROUP + y for x in even for y in (0, 2)]
    order = places + [n for m in later for n in (m, m ^ 1)]
    place = jnp.array([order.index(m) * pairs for m in range(columns)], jnp.int32)

    in_hbm = [
        pltpu.with_memory_space_constraint(value, pltpu.HBM)
        for value in (tile_source, tile_owner, dispatch_table, result_list, subspace_transfers)
    ]
    tile_list, fed, transfers = pl.pallas_call(
        functools.partial(list_kernel, columns, len(places) * pairs),
        out_shape=[
            jax.ShapeDtypeStruct((3, 4, tiles + UNROLL), jnp.int32),
            jax.ShapeDtypeStruct((half + 1, GROUP), jnp.int32),
            pltpu.VMEM(subspace_transfers.shape, jnp.bfloat16),
        ],
        in_specs=[SMEM()] * 6 + [HBM()],
        out_specs=[SMEM(), SMEM(), VMEM()],
        scratch_shapes=[pltpu.SemaphoreType.DMA],
        compiler_params=pltpu.CompilerParams(vmem_limit_bytes=16 * 2**20),
        name="tile_list",
    )(me[None], place, *in_hbm)

    work = pl.CostEstimate(
        flops=2 * tiles * width**3, bytes_accessed=tiles * width**2, transcendentals=0
    )
    totals = pl.pallas_call(
        early_kernel,
        out_shape=jax.ShapeDtypeStruct((columns // 2 + 1, width, width), jnp.float32),
        in_specs=[SMEM(), VMEM(), VMEM()],
        out_specs=VMEM(),
        compiler_params=pltpu.CompilerParams(vmem_limit_bytes=16 * 2**20),
        cost_estimate=work,
        name="early_tiles",
    )(tile_list, early, transfers)

    for x in even:
        lane[x], totals = lax.optimization_barrier((lane[x], totals))
        across[x] = jnp.concatenate(
            [swap(lane[x][: pairs // 2], 2), swap(across[x + 1][pairs // 2 :], GROUP)]
        )
    parts = {x * GROUP + 2: across[x] for x in odd}
    parts |= {x * GROUP + y: part[x] for x in even for y, part in ((0, lane), (2, across))}
    late, _ = with_other(parts)

    def sums_of(part, rows, *after):
        return pl.pallas_call(
            functools.partial(late_kernel, part),
            out_shape=jax.ShapeDtypeStruct((rows * GROUP, width, width), jnp.bfloat16),
            in_specs=[SMEM(), VMEM(), VMEM(), VMEM()] + [HBM()] * len(after),
            out_specs=VMEM(),
            scratch_shapes=[pltpu.VMEM((rows * GROUP + 1, width, width), jnp.float32)],
            compiler_params=pltpu.CompilerParams(vmem_limit_bytes=16 * 2**20),
            cost_estimate=work,
            name="late_tiles",
        )(tile_list, late, transfers, totals, *after)

    def spread(block):
        return [block[0]] + [swap(block[m], m) for m in range(1, GROUP)]

    first = spread(sums_of(1, 1))
    others = sums_of(2, half - 1, first[1])
    rows = [first] + [spread(others[i * GROUP : (i + 1) * GROUP]) for i in range(half - 1)]

    near = (g ^ jnp.arange(GROUP, dtype=jnp.int32)) < g
    stays = jnp.where(near, fed[0], -1)
    onward = jnp.concatenate([jnp.where(near, -1, fed[half])[None], fed[1:half]])
    pair_ids = jnp.arange(pairs, dtype=jnp.int32)

    def by_pair(parts, fed_pairs):
        chosen = (fed_pairs[:, None] == pair_ids)[:, :, None, None]
        terms = [jnp.where(chosen[m], parts[m].astype(jnp.float32), 0.0) for m in range(GROUP)]
        return functools.reduce(jnp.add, terms)

    coupled = []
    for row, block in enumerate(rows):
        sums = by_pair(block, onward[row]).astype(jnp.bfloat16)
        if row == 0:
            coupled.append(by_pair(block, stays))
        coupled.append(ahead(sums, row if row else half))

    base = pl.pallas_call(
        base_kernel,
        out_shape=pltpu.VMEM(amplitudes.shape, jnp.float32),
        in_specs=[SMEM(), VMEM(), VMEM(), VMEM()],
        out_specs=VMEM(),
        name="base",
    )(pno_size, energies, integrals, masked)

    total = functools.reduce(jnp.add, [part.astype(jnp.float32) for part in coupled], base)
    lanes = jnp.arange(width, dtype=jnp.int32)
    live = lanes[None, :] < pno_size[:, None]
    return jnp.where(live[:, :, None] & live[:, None, :], total, 0.0)


def solution(mesh):
    placed = (
        P(("frag", "col"), None, None),
        P(("frag", "col"), None, None),
        P(("frag", "col"), None),
        P(("frag", "col")),
        P(("frag", "col"), None, None),
        P(("frag", "col")),
        P(("frag", "col")),
        P("frag", None),
        P("frag", None),
    )
    return jax.shard_map(
        shards,
        mesh=mesh,
        in_specs=placed,
        out_specs=P(("frag", "col"), None, None),
        check_vma=False,
    )
```
